32 devices in a mesh: env: 4 (over y, x), wave: 8 (over z, core).
Axes of the slice: x: 2, y: 2, z: 4, core: 2. Of those that a mesh axis runs over, the one named last changes fastest.
Arguments:
- psi: bfloat16 [512, 128, 128], P('wave'), may hold values from -6 to 6
- left_env: bfloat16 [40, 8, 128, 128], P('env', 'wave'), may hold values from -0.5 to 0.5
- right_env: bfloat16 [40, 8, 128, 128], P('env', 'wave'), may hold values from -0.078125 to 0.078125
- left_sector: int32 [512, 1], P('wave'), may hold values from 0 to 7; in each aligned block of 64 rows (0 to 63, 64 to 127, ...) at most 16 rows name the same one
- right_sector: int32 [512, 1], P('wave'), may hold values from 0 to 7
- sector_owner: int32 [8], replicated, may hold values from 0 to 7, each once
- sector_rows: int32 [8], replicated, may hold values from 64 to 128
Outputs:
- h_psi: bfloat16 [512, 128, 128], P('wave', 'env')
The draws below stay inside these ranges and needn't reach their ends.
Inputs may be any that keep to these rules, and one draw needn't show every extreme that they name: `left_sector`: among the 64 blocks of one wave index no left sector appears more than 16 times, and some sector appears exactly 16 times. `sector_owner`: each wave index holds the environments of exactly one sector.
All inputs are finite; a program needn't handle non-finite values.
Results may differ from the reference program's by a relative error of at most 0.013.
Values may be sent and summed in bfloat16 or wider, within the bound.
No kernel may reach another device: no remote copies, remote signals or barrier semaphores. Data moves between devices by JAX's collectives and lax.ppermute only.
A program may use at most 128 MiB of HBM per device.

```python
import math
import jax
import jax.numpy as jnp
import numpy as np
from jax import lax

BLK = 128
CH = 40
PSI_DEV = 64
SECTORS = 8
CAP = 16
BLOCKS = 512
N_ENV = 4


def with_ends(drawn, rng, least, top_value):
    spot = [jax.random.randint(jax.random.fold_in(rng, axis), (), 0, length) for axis, length in enumerate(drawn.shape)]
    main_axis = drawn.shape.index(max(drawn.shape))
    neighbour = spot[:main_axis] + [(spot[main_axis] + 1) % drawn.shape[main_axis]] + spot[main_axis + 1:]
    return drawn.at[tuple(spot)].set(least).at[tuple(neighbour)].set(top_value)


def level_of(rng, shape, cuts, least, high):
    def one(dim, shards_of):
        draws = jax.random.uniform(jax.random.fold_in(jax.random.fold_in(rng, 6), dim), (shards_of,), jnp.float32, least / len(cuts), high / len(cuts))
        return jnp.repeat(jnp.exp(draws), shape[dim] // shards_of).reshape((-1,) + (1,) * (len(shape) - dim - 1))

    gain = one(*cuts[0])
    for cut in cuts[1:]:
        gain = gain * one(*cut)
    return gain


def assign_block(rng, own, number, rows, amount, top, limit, slope):
    order = jax.random.permutation(rng, amount)
    crowded, usual = shares(amount, rows * top, limit, slope, True), shares(amount, rows * top, limit, slope, False)
    places = jnp.arange(amount)

    def named(sizes, turn):
        used = int((sizes > 0).sum())
        fixed = max(1, used // 4)
        passed = fixed + (places - fixed + turn * (used - fixed)) % max(1, amount - fixed)
        return jnp.zeros((amount,), jnp.int32).at[order[jnp.where(places < fixed, places, passed)]].set(jnp.asarray(sizes, jnp.int32))

    sizes = jnp.where(number % 4 == 0, named(crowded, number // 4), named(usual, number - number // 4 - 1))
    mixed = jax.random.permutation(jax.random.fold_in(own, 3), amount)
    donor, taker = mixed[0:amount // 2 * 2:2], mixed[1:amount // 2 * 2:2]
    room = jnp.minimum(sizes[donor] - 1, limit - sizes[taker]) // 2
    room = jnp.where((donor == order[0]) | (taker == order[0]) | (sizes[taker] == 0), 0, jnp.maximum(room, 0))
    passed = jax.random.randint(jax.random.fold_in(own, 4), (amount // 2,), 0, 1 << 20) % (room + 1)
    sizes = sizes.at[donor].add(-passed).at[taker].add(passed)
    items = jnp.searchsorted(jnp.cumsum(sizes), jnp.arange(rows * top), side="right").astype(jnp.int32)
    table = items.reshape(top, rows).T
    table = table[jax.random.permutation(jax.random.fold_in(own, 1), rows)]
    turn = jax.random.randint(jax.random.fold_in(own, 2), (rows, 1), 0, top)
    return jnp.take_along_axis(table, (jnp.arange(top)[None, :] + turn) % top, axis=1)


def shares(amount, total, bound, slope, full):
    weights = [(1 << 20) // math.isqrt(rank ** slope) + 1 for rank in range(1, amount + 1)]
    largest = bound if full else min(bound, max(-(-total // amount), total * weights[0] // sum(weights)))
    least = 1 if total - largest >= amount - 1 else 0
    given, rest = [largest] + [least] * (amount - 1), total - largest - least * (amount - 1)
    while rest > 0:
        candidates = [i for i in range(1, amount) if given[i] < largest] or [i for i in range(1, amount) if given[i] < bound]
        mass, left = sum([weights[i] for i in candidates]), rest
        for i in candidates:
            extra = min(bound - given[i], max(1, left * weights[i] // mass), rest)
            given[i] = given[i] + extra
            rest = rest - extra
    return np.array(given)


def bell_draw(stream_key, dims, spread, most, pieces=(), kind=jnp.bfloat16):
    entries = jax.random.normal(stream_key, dims, jnp.float32) * spread
    if len(pieces) > 0:
        entries = level_of(stream_key, dims, pieces, -0.22, 0.18) * entries
    return jnp.clip(entries, min=-most, max=most).astype(kind)


def setup_inputs(seed: int = 0) -> dict:
    arg_keys = jax.random.split(jax.random.key(seed), 8)
    psi = bell_draw(arg_keys[0], (BLOCKS, BLK, BLK), 1.0, 6.0, ((0, 8),))
    left_env = bell_draw(arg_keys[1], (CH, SECTORS, BLK, BLK), BLK ** -0.5, 0.5, ((0, 4), (1, 8)))
    right_env = bell_draw(arg_keys[2], (CH, SECTORS, BLK, BLK), (BLK * CH) ** -0.5, 0.078125, ((0, 4), (1, 8)))
    left_sector_keys = jax.random.split(jax.random.fold_in(arg_keys[3], 1), BLOCKS // PSI_DEV)
    left_sector_turns = jax.random.permutation(jax.random.fold_in(arg_keys[3], 3), BLOCKS // PSI_DEV)
    left_sector = jax.vmap(lambda own, number: assign_block(jax.random.fold_in(arg_keys[3], 2), own, number, PSI_DEV, SECTORS, 1, CAP, 2))(left_sector_keys, left_sector_turns).reshape((BLOCKS, 1))
    right_sector = with_ends(jax.random.randint(arg_keys[4], (BLOCKS, 1), 0, SECTORS), jax.random.fold_in(arg_keys[4], 1), 0, SECTORS - 1).astype(jnp.int32)
    sector_owner = jax.random.permutation(arg_keys[5], SECTORS).astype(jnp.int32)
    sector_rows = with_ends(jax.random.randint(arg_keys[6], (SECTORS,), BLK // 2, BLK + 1), jax.random.fold_in(arg_keys[6], 1), BLK // 2, BLK).astype(jnp.int32)
    return {"psi": psi, "left_env": left_env, "right_env": right_env, "left_sector": left_sector, "right_sector": right_sector, "sector_owner": sector_owner, "sector_rows": sector_rows}


def reference(psi, left_env, right_env, left_sector, right_sector, sector_owner, sector_rows):
    group = CH // N_ENV
    lsec = left_sector[:, 0].astype(jnp.int32)
    rsec = right_sector[:, 0].astype(jnp.int32)
    lpos = sector_owner[lsec].astype(jnp.int32)
    rpos = sector_owner[rsec].astype(jnp.int32)
    lrows = sector_rows[lsec].astype(jnp.int32)
    rrows = sector_rows[rsec].astype(jnp.int32)
    line = jnp.arange(BLK, dtype=jnp.int32)

    def one_block(items):
        block, lplace, rplace, lcount, rcount = items
        mask = (line[:, None] < lcount) & (line[None, :] < rcount)
        masked = jnp.where(mask, block, jnp.zeros_like(block))
        lmats = jnp.take(left_env, lplace, axis=1)
        rmats = jnp.take(right_env, rplace, axis=1)
        inner = jnp.einsum("wab,bc->wac", lmats.astype(jnp.float32), masked.astype(jnp.float32))
        inner = inner.astype(jnp.bfloat16)
        terms = jnp.einsum("wac,wcd->wad", inner.astype(jnp.float32), rmats.astype(jnp.float32))
        parts = jnp.sum(terms.reshape(N_ENV, group, BLK, BLK), axis=1).astype(jnp.bfloat16)
        total = jnp.sum(parts.astype(jnp.float32), axis=0)
        return jnp.where(mask, total, jnp.zeros_like(total)).astype(jnp.bfloat16)

    return lax.map(one_block, (psi, lpos, rpos, lrows, rrows))
```

```python
import functools

import jax
import jax.numpy as jnp
from jax import lax
from jax.experimental import pallas as pl
from jax.experimental.pallas import tpu as pltpu
from jax.sharding import PartitionSpec as P

CORES = 2
PARTS = 4


def block_kernel(unroll, first, nenv, chips, place, lsec, rsec, owner, live, psi, envs, out):
    blocks, width = out.shape[1], psi.shape[1]
    share = width // nenv
    channels = envs.shape[1] // 2
    chip, core, env = place[0], place[1], place[2]
    row = lax.broadcasted_iota(jnp.int32, (width, width), 0)
    col = lax.broadcasted_iota(jnp.int32, (width, width), 1)

    def slot_of(sector):
        where = owner[sector]
        away = lax.rem(where // CORES - chip + chips, chips)
        return away * CORES + lax.rem(where + core, CORES)

    def one(k):
        left, right = lsec[first + k], rsec[first + k]
        lslot, rslot = slot_of(left), slot_of(right)
        mask = (row < live[left]) & (col < live[right])
        block = psi[first + k]
        block = jnp.where(mask, block, jnp.zeros_like(block))
        lmat = envs[lslot, 0:channels].reshape(channels * width, width)
        y = jnp.dot(lmat, block, preferred_element_type=jnp.float32).astype(jnp.bfloat16)
        wide = jnp.concatenate([y[w * width:(w + 1) * width] for w in range(channels)], axis=1)
        rmat = envs[rslot, channels:2 * channels].reshape(channels * width, width)
        part = jnp.dot(wide, rmat, preferred_element_type=jnp.float32)
        part = jnp.where(mask, part, jnp.zeros_like(part)).astype(jnp.bfloat16)
        for e in range(nenv):
            out[env ^ e, k] = part[e * share:(e + 1) * share]

    def body(g, carry):
        for u in range(unroll):
            one(g * unroll + u)
        return carry

    lax.fori_loop(0, blocks // unroll, body, 0)


def on_device(psi, left_env, right_env, left_sector, right_sector, sector_owner, sector_rows):
    nwave = lax.axis_size("wave")
    nenv = lax.axis_size("env")
    count, width = psi.shape[0], psi.shape[1]
    channels = left_env.shape[0]
    chips = nwave // CORES
    wave = lax.axis_index("wave")
    env = lax.axis_index("env")
    place = jnp.stack([wave // CORES, wave % CORES, env]).astype(jnp.int32)

    up = [(i, (i + CORES) % nwave) for i in range(nwave)]
    down = [((i + CORES) % nwave, i) for i in range(nwave)]
    other = [(i, i ^ 1) for i in range(nwave)]
    swap = lambda x: lax.ppermute(x, "wave", other)

    own = jnp.concatenate([left_env[:, 0], right_env[:, 0]], axis=0)
    held = [[None, None] for _ in range(chips)]
    held[0] = [own, swap(own)]
    rising = falling = own
    for r in range(1, (chips - 1) // 2 + 1):
        rising = lax.ppermute(rising, "wave", up)
        falling = lax.ppermute(falling, "wave", down)
        held[chips - r] = [rising, swap(rising)]
        held[r] = [falling, swap(falling)]
    if chips % 2 == 0 and chips > 1:
        far_left = lax.ppermute(rising[:channels], "wave", up)
        far_right = lax.ppermute(falling[channels:], "wave", down)
        far = jnp.concatenate([far_left, far_right], axis=0)
        far_other = jnp.concatenate([swap(far_left), swap(far_right)], axis=0)
        held[chips // 2] = [far, far_other]
    envs = jnp.stack([piece for pair in held for piece in pair])

    blocks = count // PARTS
    smem = pl.BlockSpec(memory_space=pltpu.SMEM)
    vmem = pl.BlockSpec(memory_space=pltpu.VMEM)
    results = []
    for part in range(PARTS):
        sums = pl.pallas_call(
            functools.partial(block_kernel, 4, part * blocks, nenv, chips),
            out_shape=jax.ShapeDtypeStruct((nenv, blocks, width // nenv, width), jnp.bfloat16),
            in_specs=[smem] * 5 + [vmem] * 2,
            out_specs=vmem,
            compiler_params=pltpu.CompilerParams(vmem_limit_bytes=56 << 20),
            cost_estimate=pl.CostEstimate(
                flops=4 * blocks * channels * width ** 3, bytes_accessed=8 << 20, transcendentals=0
            ),
        )(place, left_sector[:, 0], right_sector[:, 0], sector_owner, sector_rows, psi, envs)
        total = sums[0].astype(jnp.float32)
        for d in range(1, nenv):
            total = total + lax.ppermute(sums[d], "env", [(i, i ^ d) for i in range(nenv)]).astype(jnp.float32)
        results.append(total.astype(jnp.bfloat16))
    return jnp.concatenate(results, axis=0)


def solution(mesh):
    return jax.shard_map(
        on_device,
        mesh=mesh,
        in_specs=(
            P("wave", None, None),
            P("env", "wave", None, None),
            P("env", "wave", None, None),
            P("wave", None),
            P("wave", None),
            P(),
            P(),
        ),
        out_specs=P("wave", "env", None),
        check_vma=False,
    )
```

```python
import functools

import jax
import jax.numpy as jnp
from jax import lax
from jax.experimental import pallas as pl
from jax.experimental.pallas import tpu as pltpu
from jax.sharding import PartitionSpec as P

CORES = 2
STACK = 4
SPLIT = 2
UNROLL = 6
NO_COST = pl.CostEstimate(flops=0, bytes_accessed=0, transcendentals=0)
SMEM = pl.BlockSpec(memory_space=pltpu.SMEM)
VMEM = pl.BlockSpec(memory_space=pltpu.VMEM)


def padded(n):
    return (n + UNROLL - 1) // UNROLL * UNROLL


class Lists:
    def __init__(self, blocks, sectors):
        used = min(sectors, blocks)
        self.blocks = blocks
        self.pairs = padded((blocks + used) // 2)
        self.groups = padded(min(blocks, (blocks + (STACK - 1) * used) // STACK))
        self.pair_slot = 2
        self.pair_pos = self.pair_slot + self.pairs
        self.group_slot = self.pair_pos + 2 * self.pairs
        self.group_start = self.group_slot + self.groups
        self.group_block = self.group_start + self.groups
        self.length = self.group_block + STACK * self.groups


def cut_kernel(groups, place, left, right, out):
    channels, width, rows = right.shape[0], right.shape[1], out.shape[1]
    for q in range(width // rows):
        for w in range(channels):
            out[w * (width // rows) + q] = right[w, q * rows:(q + 1) * rows, :]
    base = channels * (width // rows)
    for group in groups:
        for i, d in enumerate(group):
            start = pl.multiple_of((place[2] ^ d) * rows, rows)
            for w in range(channels):
                out[base + w * len(group) + i] = left[w, pl.ds(start, rows), :]
        base = base + channels * len(group)


def order_kernel(
    chips, at, place, lsec, rsec, owner, live, psi, lists, halves, lcount, rcount, lbase, rbase, rfirst, lrank, rrank, origin
):
    width = psi.shape[1]
    sectors = owner.shape[0]
    chip, core = place[0], place[1]
    row = lax.broadcasted_iota(jnp.int32, (width, width), 0)
    col = lax.broadcasted_iota(jnp.int32, (width, width), 1)
    zero = jnp.int32(0)

    def slot_of(sector):
        where = owner[sector]
        away = lax.rem(where // CORES - chip + chips, chips)
        return away * CORES + lax.rem(where + core, CORES)

    for part in range(SPLIT):
        base = part * at.length
        start = part * at.blocks

        def clear_sector(s, carry):
            lcount[s] = 0
            rcount[s] = 0
            return carry

        def clear_pair(p, carry):
            lists[base + at.pair_slot + p] = 0
            for h in range(2):
                lists[base + at.pair_pos + 2 * p + h] = at.blocks
                origin[2 * p + h] = 0
            return carry

        def clear_group(g, carry):
            lists[base + at.group_slot + g] = 0
            lists[base + at.group_start + g] = 0
            for j in range(STACK):
                lists[base + at.group_block + STACK * g + j] = at.blocks
            return carry

        def count(k, carry):
            left, right = lsec[start + k], rsec[start + k]
            lrank[k] = lcount[left]
            rrank[k] = rcount[right]
            lcount[left] = lcount[left] + 1
            rcount[right] = rcount[right] + 1
            return carry

        def bases(s, carry):
            pair, group, first = carry
            lbase[s] = pair
            rbase[s] = group
            rfirst[s] = first
            return pair + (lcount[s] + 1) // 2, group + (rcount[s] + STACK - 1) // STACK, first + rcount[s]

        def enter(k, carry):
            left, right = lsec[start + k], rsec[start + k]
            lr, rr = lrank[k], rrank[k]
            position = rfirst[right] + rr
            place_in = lax.rem(rr, STACK)
            group = rbase[right] + rr // STACK
            lists[base + at.group_slot + group] = slot_of(right)
            lists[base + at.group_start + group] = position - place_in
            lists[base + at.group_block + STACK * group + place_in] = k
            pair = lbase[left] + lr // 2
            lists[base + at.pair_slot + pair] = slot_of(left)
            lists[base + at.pair_pos + 2 * pair + lax.rem(lr, 2)] = position
            origin[2 * pair + lax.rem(lr, 2)] = k
            return carry

        lax.fori_loop(0, sectors, clear_sector, 0)
        lax.fori_loop(0, at.pairs, clear_pair, 0)
        lax.fori_loop(0, at.groups, clear_group, 0)
        lax.fori_loop(0, at.blocks, count, 0)
        pairs, groups, _ = lax.fori_loop(0, sectors, bases, (zero, zero, zero))
        lists[base] = (pairs + UNROLL - 1) // UNROLL
        lists[base + 1] = (groups + UNROLL - 1) // UNROLL
        lax.fori_loop(0, at.blocks, enter, 0)

        def fill(p, carry):
            for h in range(2):
                k = start + origin[2 * p + h]
                mask = (row < live[lsec[k]]) & (col < live[rsec[k]])
                block = psi[k]
                halves[part * at.pairs + p, :, h * width:(h + 1) * width] = jnp.where(mask, block, jnp.zeros_like(block))
            return carry

        lax.fori_loop(0, lists[base] * UNROLL, fill, 0)


def multiply_kernel(rows, first_chunk, parts, at, lists, halves, right, left, *rest):
    outs, inner = rest[:-1], rest[-1]
    width = halves.shape[1]
    span = inner.shape[1]
    channels = inner.shape[2] // width
    chunks = channels * span // rows
    spare = len(parts) * at.blocks

    for number, part in enumerate(parts):
        base = part * at.length

        def first(p):
            lmat = left[lists[base + at.pair_slot + p], first_chunk:first_chunk + chunks].reshape(channels * span, width)
            y = jnp.dot(lmat, halves[part * at.pairs + p], preferred_element_type=jnp.float32).astype(jnp.bfloat16)
            for h in range(2):
                where = lists[base + at.pair_pos + 2 * p + h]
                for w in range(channels):
                    inner[where, :, w * width:(w + 1) * width] = (
                        y[w * span:(w + 1) * span, h * width:(h + 1) * width]
                    )

        def second(g):
            rmat = right[lists[base + at.group_slot + g], 0:channels * width // rows].reshape(channels * width, width)
            stack = inner[pl.ds(lists[base + at.group_start + g], STACK)].reshape(STACK * span, channels * width)
            part_sum = jnp.dot(stack, rmat, preferred_element_type=jnp.float32).astype(jnp.bfloat16)
            for j in range(STACK):
                block = lists[base + at.group_block + STACK * g + j]
                block = jnp.where(block == at.blocks, spare, block + number * at.blocks)
                for i, out in enumerate(outs):
                    out[block] = part_sum[j * span + i * rows:j * span + (i + 1) * rows]

        def loop(step, trips):
            def body(i, carry):
                for u in range(UNROLL):
                    step(i * UNROLL + u)
                return carry

            lax.fori_loop(0, trips, body, 0)

        loop(first, lists[base])
        loop(second, lists[base + 1])


def sum_kernel(part, nenv, place, lsec, rsec, live, *rest):
    out, terms = rest[-1], rest[:nenv]
    blocks, rows, width = out.shape
    row = place[2] * rows + lax.broadcasted_iota(jnp.int32, (rows, width), 0)
    col = lax.broadcasted_iota(jnp.int32, (rows, width), 1)

    def body(k, carry):
        total = terms[0][k].astype(jnp.float32)
        for term in terms[1:]:
            total = total + term[k].astype(jnp.float32)
        mask = (row < live[lsec[part * blocks + k]]) & (col < live[rsec[part * blocks + k]])
        out[k] = jnp.where(mask, total, jnp.zeros_like(total)).astype(jnp.bfloat16)
        return carry

    lax.fori_loop(0, blocks, body, 0, unroll=8)


def on_device(psi, left_env, right_env, left_sector, right_sector, sector_owner, sector_rows):
    nwave = lax.axis_size("wave")
    nenv = lax.axis_size("env")
    count, width = psi.shape[0], psi.shape[1]
    channels = left_env.shape[0]
    sectors = sector_owner.shape[0]
    chips = nwave // CORES
    rows = width // nenv
    wave = lax.axis_index("wave")
    env = lax.axis_index("env")
    place = jnp.stack([wave // CORES, wave % CORES, env]).astype(jnp.int32)
    lsec, rsec = left_sector[:, 0], right_sector[:, 0]

    up = [(i, (i + CORES) % nwave) for i in range(nwave)]
    down = [((i + CORES) % nwave, i) for i in range(nwave)]
    other = [(i, i ^ 1) for i in range(nwave)]
    half = channels // 2
    swap = lambda x: lax.ppermute(x, "wave", other)

    def gate(*values):
        return lax.optimization_barrier(values)

    def ring(own):
        held = {0: own}
        rising = falling = own
        for r in range(1, (chips - 1) // 2 + 1):
            rising = lax.ppermute(rising, "wave", up)
            falling = lax.ppermute(falling, "wave", down)
            held[chips - r], held[r] = rising, falling
        return held, rising, falling

    def far(rising, falling, lo, hi):
        mid = (lo + hi) // 2
        return [lax.ppermute(rising[lo:mid], "wave", up), lax.ppermute(falling[mid:hi], "wave", down)]

    def stack(held, others, last, lo, hi):
        pieces = []
        for d in range(chips):
            if d in held:
                pieces += [held[d][lo:hi], others[d][lo:hi]]
            else:
                pieces += [jnp.concatenate(last), jnp.concatenate([swap(x) for x in last])]
        return jnp.stack(pieces)

    at = Lists(count // SPLIT, sectors)
    scratch = lambda n: pltpu.SMEM((n,), jnp.int32)
    lists, halves = pl.pallas_call(
        functools.partial(order_kernel, chips, at),
        out_shape=(
            jax.ShapeDtypeStruct((SPLIT * at.length,), jnp.int32),
            jax.ShapeDtypeStruct((SPLIT * at.pairs, width, 2 * width), jnp.bfloat16),
        ),
        in_specs=[SMEM] * 5 + [VMEM],
        out_specs=(SMEM, VMEM),
        scratch_shapes=[scratch(sectors)] * 5 + [scratch(at.blocks)] * 2 + [scratch(2 * at.pairs)],
    )(place, lsec, rsec, sector_owner, sector_rows, psi)

    def multiply(right, left, first_chunk, number, parts):
        span = number * rows
        blocks = len(parts) * at.blocks
        need = right.size + left.size + halves.size + (at.blocks + STACK) * span * channels * width
        need = 2 * (need + number * (blocks + 1) * rows * width) + (8 << 20)
        return pl.pallas_call(
            functools.partial(multiply_kernel, rows, first_chunk, parts, at),
            out_shape=[jax.ShapeDtypeStruct((blocks + 1, rows, width), jnp.bfloat16)] * number,
            in_specs=[SMEM] + [VMEM] * 3,
            out_specs=[VMEM] * number,
            scratch_shapes=[pltpu.VMEM((at.blocks + STACK, span, channels * width), jnp.bfloat16)],
            compiler_params=pltpu.CompilerParams(vmem_limit_bytes=min(need, 60 << 20)),
            cost_estimate=NO_COST,
        )(lists, halves, right, left)

    def send(x, d):
        return lax.ppermute(x[:-1], "env", [(i, i ^ d) for i in range(nenv)])

    lead, *rest = range(nenv - 1, 0, -1)
    everything = tuple(range(SPLIT))
    quarters = channels * nenv
    lead_end = quarters + channels
    rest_end = lead_end + channels * len(rest)
    end = rest_end + channels
    own = pl.pallas_call(
        functools.partial(cut_kernel, ([lead], rest, [0])),
        out_shape=jax.ShapeDtypeStruct((end, rows, width), jnp.bfloat16),
        in_specs=[SMEM, VMEM, VMEM],
        out_specs=VMEM,
    )(place, left_env[:, 0], right_env[:, 0])
    held, rising, falling = ring(own)
    others = {d: swap(x) for d, x in held.items()}
    last_one = far(rising, falling, 0, lead_end)
    last_two = far(rising, falling, lead_end, end)
    one = stack(held, others, last_one, 0, lead_end)
    two = stack(held, others, last_two, lead_end, end)
    here = [[] for _ in range(nenv)]
    for part in everything:
        (sums,) = multiply(one, one, quarters, 1, (part,))
        if part == SPLIT - 1:
            sums, two = gate(sums, two)
        here[lead].append(send(sums, lead))
    for part in everything:
        if part > 0:
            two, here[lead][part - 1] = gate(two, here[lead][part - 1])
        parts = multiply(one, two, 0, len(rest), (part,))
        if part == SPLIT - 1:
            *parts, two = gate(*parts, two)
        for x, d in zip(parts, rest):
            here[d].append(send(x, d))
    for part in everything:
        for d in [lead] if part == 0 else rest:
            at_part = SPLIT - 1 if part == 0 else part - 1
            two, here[d][at_part] = gate(two, here[d][at_part])
        here[0].append(multiply(one, two, rest_end - lead_end, 1, (part,))[0])

    out_shape = jax.ShapeDtypeStruct((count, rows, width), jnp.bfloat16)
    total = None
    for part in everything:
        args = [place, lsec, rsec, sector_rows] + [here[d][part] for d in range(nenv)]
        specs = [SMEM] * 4 + [VMEM] * nenv
        alias = {}
        if total is not None:
            alias = {len(args): 0}
            args.append(total)
            specs.append(pl.BlockSpec(memory_space=pl.ANY))
        total = pl.pallas_call(
            functools.partial(sum_kernel, part, nenv),
            grid=(1,),
            out_shape=out_shape,
            in_specs=specs,
            out_specs=pl.BlockSpec((at.blocks, rows, width), lambda i, part=part: (part, 0, 0)),
            input_output_aliases=alias,
        )(*args)
    return total


def solution(mesh):
    return jax.shard_map(
        on_device,
        mesh=mesh,
        in_specs=(
            P("wave", None, None),
            P("env", "wave", None, None),
            P("env", "wave", None, None),
            P("wave", None),
            P("wave", None),
            P(),
            P(),
        ),
        out_specs=P("wave", "env", None),
        check_vma=False,
    )
```

```python
import functools

import jax
import jax.numpy as jnp
from jax import lax
from jax.experimental import pallas as pl
from jax.experimental.pallas import tpu as pltpu
from jax.sharding import PartitionSpec as P

CORES = 2
DEPTH = 2
PARTS = (2, 2)
BATCH = 8
NO_COST = pl.CostEstimate(flops=0, bytes_accessed=0, transcendentals=0)
SMEM = pl.BlockSpec(memory_space=pltpu.SMEM)
VMEM = pl.BlockSpec(memory_space=pltpu.VMEM)


class Lists:
    def __init__(self, count, sectors, chips):
        self.count = count
        self.sectors = sectors
        self.chips = chips
        self.sizes = [count // n for n in PARTS]
        self.starts = [sum(self.sizes[:i]) for i in range(len(PARTS))]
        self.pairs = [((n + min(sectors, n)) // 2 + DEPTH - 1) // DEPTH * DEPTH for n in self.sizes]
        self.firsts = [sum(self.pairs[:i]) for i in range(len(PARTS))]
        self.all_pairs = sum(self.pairs)
        self.far = chips // 2 if chips % 2 == 0 else chips
        self.groups = 0
        self.left = self.groups + len(PARTS)
        self.right = self.left + self.all_pairs
        self.position = self.right + 2 * self.all_pairs
        self.origin = self.position + 2 * self.all_pairs
        self.rows = self.origin + count
        self.columns = self.rows + count
        self.length = self.columns + count


def order_kernel(at, place, lsec, rsec, owner, live, psi, lists, halves, base, rank, source):
    width = psi.shape[1]
    chips = at.chips
    chip, core = place[0], place[1]
    row = lax.broadcasted_iota(jnp.int32, (width, width), 0)
    col = lax.broadcasted_iota(jnp.int32, (width, width), 1)
    zero = jnp.int32(0)

    def slot_of(sector):
        where = owner[sector]
        away = lax.rem(where // CORES - chip + chips, chips)
        away = jnp.where(away == at.far, chips - 1, jnp.where(away > at.far, away - 1, away))
        return away * CORES + lax.rem(where + core, CORES)

    def clear_slot(s, carry):
        base[s] = 0
        return carry

    def count(k, carry):
        slot = slot_of(lsec[k])
        rank[k] = base[slot]
        base[slot] = base[slot] + 1
        return carry

    def begin(s, first):
        members = base[s]
        base[s] = first
        return first + members

    def enter(k, carry):
        lists[at.origin + base[slot_of(lsec[k])] + rank[k]] = k
        return carry

    lax.fori_loop(0, at.sectors, clear_slot, 0)
    lax.fori_loop(0, at.count, count, 0)
    lax.fori_loop(0, at.sectors, begin, zero)
    lax.fori_loop(0, at.count, enter, 0)

    for part, (start, size, first) in enumerate(zip(at.starts, at.sizes, at.firsts)):
        def clear_pair(p, carry):
            lists[at.left + p] = 0
            for h in range(2):
                lists[at.right + 2 * p + h] = 0
                lists[at.position + 2 * p + h] = size
                source[2 * p + h] = 0
            return carry

        def pair_up(i, carry):
            pair, filled, before = carry
            k = lists[at.origin + start + i]
            left, right = lsec[k], rsec[k]
            same = (filled == 1) & (left == before)
            pair = jnp.where(same, pair, pair + 1)
            filled = jnp.where(same, 2, 1)
            half = 2 * pair + filled - 1
            lists[at.left + pair] = slot_of(left)
            lists[at.right + half] = slot_of(right)
            lists[at.position + half] = i
            lists[at.rows + start + i] = live[left]
            lists[at.columns + start + i] = live[right]
            source[half] = k
            return pair, filled, left

        lax.fori_loop(first, first + at.pairs[part], clear_pair, 0)
        last, _, _ = lax.fori_loop(0, size, pair_up, (zero + first - 1, zero, zero - 1))
        groups = (last - first + DEPTH) // DEPTH
        lists[at.groups + part] = groups

        def fill(i, carry):
            for u in range(DEPTH):
                p = first + i * DEPTH + u
                for h in range(2):
                    k = source[2 * p + h]
                    mask = (row < live[lsec[k]]) & (col < live[rsec[k]])
                    block = psi[k]
                    halves[p, :, h * width:(h + 1) * width] = jnp.where(mask, block, jnp.zeros_like(block))
            return carry

        lax.fori_loop(0, groups, fill, 0)


def multiply_kernel(part, at, place, lists, halves, right, left, *rest):
    outs, inner = rest[:-1], rest[-1]
    width = halves.shape[1]
    rows = outs[0].shape[1]
    channels = left.shape[1]
    first = at.firsts[part]
    groups = lists[at.groups + part]

    def one(group, side):
        for u in range(DEPTH):
            pair = first + group * DEPTH + u
            for h in range(2):
                slot = lists[at.right + 2 * pair + h]
                wide = jnp.concatenate([right[slot, w] for w in range(channels)], axis=1)
                block = halves[pair, :, h * width:(h + 1) * width]
                z = jnp.dot(block, wide, preferred_element_type=jnp.float32).astype(jnp.bfloat16)
                for w in range(channels):
                    inner[side * DEPTH + u, w * width:(w + 1) * width, h * width:(h + 1) * width] = (
                        z[:, w * width:(w + 1) * width]
                    )

    def two(group, side):
        for u in range(DEPTH):
            pair = first + group * DEPTH + u
            slot = lists[at.left + pair]
            wide = []
            for d in range(len(outs)):
                start = pl.multiple_of((place[2] ^ d) * rows, rows)
                wide.append(jnp.concatenate([left[slot, w, pl.ds(start, rows), :] for w in range(channels)], axis=1))
            wide = jnp.concatenate(wide, axis=0)
            result = jnp.dot(wide, inner[side * DEPTH + u], preferred_element_type=jnp.float32).astype(jnp.bfloat16)
            for h in range(2):
                where = lists[at.position + 2 * pair + h]
                for d, out in enumerate(outs):
                    out[where] = result[d * rows:(d + 1) * rows, h * width:(h + 1) * width]

    def body(i, carry):
        one(2 * i + 1, 1)
        two(2 * i, 0)
        one(2 * i + 2, 0)
        two(2 * i + 1, 1)
        return carry

    one(0, 0)
    turns = (groups - 1) // 2
    lax.fori_loop(0, turns, body, 0)

    @pl.when(2 * turns + 1 == groups)
    def _():
        two(2 * turns, 0)

    @pl.when(2 * turns + 1 != groups)
    def _():
        one(2 * turns + 1, 1)
        two(2 * turns, 0)
        two(2 * turns + 1, 1)


def place_kernel(at, place, lists, *rest):
    out, totals = rest[-1], rest[:-1]
    rows, width = out.shape[1], out.shape[2]
    row = place[2] * rows + lax.broadcasted_iota(jnp.int32, (rows, width), 0)
    col = lax.broadcasted_iota(jnp.int32, (rows, width), 1)

    for start, total in zip(at.starts, totals):
        def body(i, carry):
            blocks = []
            for u in range(BATCH):
                k = start + i * BATCH + u
                mask = (row < lists[at.rows + k]) & (col < lists[at.columns + k])
                block = total[i * BATCH + u].astype(jnp.float32)
                blocks.append(jnp.where(mask, block, jnp.zeros_like(block)).astype(jnp.bfloat16))
            for u in range(BATCH):
                out[lists[at.origin + start + i * BATCH + u]] = blocks[u]
            return carry

        lax.fori_loop(0, total.shape[0] // BATCH, body, 0)


def on_device(psi, left_env, right_env, left_sector, right_sector, sector_owner, sector_rows):
    nwave = lax.axis_size("wave")
    nenv = lax.axis_size("env")
    count, width = psi.shape[0], psi.shape[1]
    channels = left_env.shape[0]
    sectors = sector_owner.shape[0]
    chips = nwave // CORES
    rows = width // nenv
    wave = lax.axis_index("wave")
    env = lax.axis_index("env")
    place = jnp.stack([wave // CORES, wave % CORES, env]).astype(jnp.int32)

    up = [(i, (i + CORES) % nwave) for i in range(nwave)]
    down = [((i + CORES) % nwave, i) for i in range(nwave)]
    other = [(i, i ^ 1) for i in range(nwave)]
    at = Lists(count, sectors, chips)

    def swap(x):
        return lax.ppermute(x, "wave", other)

    def gate(*values):
        return lax.optimization_barrier(values)

    def ring(own):
        held = {0: own}
        rising = falling = own
        for r in range(1, (chips - 1) // 2 + 1):
            rising = lax.ppermute(rising, "wave", up)
            falling = lax.ppermute(falling, "wave", down)
            held[chips - r], held[r] = rising, falling
        return held, rising, falling

    def far(rising, falling, lo, hi):
        mid = (lo + hi) // 2
        return [lax.ppermute(rising[lo:mid], "wave", up), lax.ppermute(falling[mid:hi], "wave", down)]

    def far_pieces(last):
        return [jnp.concatenate(last), jnp.concatenate([swap(x) for x in last])]

    held, rising, falling = ring(jnp.concatenate([right_env[:, 0], left_env[:, 0]]))
    pieces = [piece for d in range(chips) if d in held for piece in (held[d], swap(held[d]))]
    right = [piece[:channels] for piece in pieces]
    near = jnp.stack([piece[channels:] for piece in pieces])
    if chips % 2 == 0:
        right += far_pieces(far(rising, falling, 0, channels))
        last = far(rising, falling, channels, 2 * channels)
    right = jnp.stack(right)

    lists, halves = pl.pallas_call(
        functools.partial(order_kernel, at),
        out_shape=(
            jax.ShapeDtypeStruct((at.length,), jnp.int32),
            jax.ShapeDtypeStruct((at.all_pairs, width, 2 * width), jnp.bfloat16),
        ),
        in_specs=[SMEM] * 5 + [VMEM],
        out_specs=(SMEM, VMEM),
        scratch_shapes=[pltpu.SMEM((n,), jnp.int32) for n in (sectors, count, 2 * at.all_pairs)],
        compiler_params=pltpu.CompilerParams(vmem_limit_bytes=2 * (psi.size + 2 * at.all_pairs * width * width) + (4 << 20)),
    )(place, left_sector[:, 0], right_sector[:, 0], sector_owner, sector_rows, psi)

    def multiply(part, right, left):
        need = right.size + left.size + halves.size + count * width * width
        need = 2 * (need + 4 * DEPTH * channels * width * width) + (8 << 20)
        return list(pl.pallas_call(
            functools.partial(multiply_kernel, part, at),
            out_shape=[jax.ShapeDtypeStruct((at.sizes[part] + 1, rows, width), jnp.bfloat16)] * nenv,
            in_specs=[SMEM] * 2 + [VMEM] * 3,
            out_specs=[VMEM] * nenv,
            scratch_shapes=[pltpu.VMEM((2 * DEPTH, channels * width, 2 * width), jnp.bfloat16)],
            compiler_params=pltpu.CompilerParams(vmem_limit_bytes=min(need, 60 << 20)),
            cost_estimate=NO_COST,
        )(place, lists, halves, right, left))

    def exchange(parts):
        total = parts[0][:-1].astype(jnp.float32)
        for d in range(nenv - 1, 0, -1):
            arrived = lax.ppermute(parts[d][:-1], "env", [(i, i ^ d) for i in range(nenv)])
            total = total + arrived.astype(jnp.float32)
        return total.astype(jnp.bfloat16)

    parts = multiply(0, right, near)
    if chips % 2 == 0:
        parts[0], *last = gate(parts[0], *last)
        whole = jnp.concatenate([near, jnp.stack(far_pieces(last))])
    else:
        whole = near
    terms = [exchange(parts)]
    for part in range(1, len(PARTS)):
        terms.append(exchange(multiply(part, right, whole)))
    return pl.pallas_call(
        functools.partial(place_kernel, at),
        out_shape=jax.ShapeDtypeStruct((count, rows, width), jnp.bfloat16),
        in_specs=[SMEM] * 2 + [VMEM] * len(terms),
        out_specs=VMEM,
        compiler_params=pltpu.CompilerParams(vmem_limit_bytes=4 * count * rows * width + (4 << 20)),
        cost_estimate=NO_COST,
    )(place, lists, *terms)


def solution(mesh):
    return jax.shard_map(
        on_device,
        mesh=mesh,
        in_specs=(
            P("wave", None, None),
            P("env", "wave", None, None),
            P("env", "wave", None, None),
            P("wave", None),
            P("wave", None),
            P(),
            P(),
        ),
        out_specs=P("wave", "env", None),
        check_vma=False,
    )
```

```python
import functools

import jax
import jax.numpy as jnp
from jax import lax
from jax.experimental import pallas as pl
from jax.experimental.pallas import tpu as pltpu
from jax.sharding import PartitionSpec as P

CORES = 2
DEPTH = 2
PARTS = (2, 2)
BATCH = 8
NO_COST = pl.CostEstimate(flops=0, bytes_accessed=0, transcendentals=0)
SMEM = pl.BlockSpec(memory_space=pltpu.SMEM)
VMEM = pl.BlockSpec(memory_space=pltpu.VMEM)


class Lists:
    def __init__(self, count, sectors, chips):
        self.count = count
        self.sectors = sectors
        self.chips = chips
        self.sizes = [count // n for n in PARTS]
        self.starts = [sum(self.sizes[:i]) for i in range(len(PARTS))]
        self.pairs = [((n + min(sectors, n) + 2) // 2 + DEPTH - 1) // DEPTH * DEPTH for n in self.sizes]
        self.firsts = [sum(self.pairs[:i]) for i in range(len(PARTS))]
        self.all_pairs = sum(self.pairs)
        self.far = chips // 2 if chips % 2 == 0 else chips
        self.groups = 0
        self.left = self.groups + len(PARTS)
        self.right = self.left + self.all_pairs
        self.position = self.right + 2 * self.all_pairs
        self.origin = self.position + 2 * self.all_pairs
        self.rows = self.origin + count
        self.columns = self.rows + count
        self.length = self.columns + count


def order_kernel(at, place, lsec, rsec, owner, live, psi, lists, halves, base, rank, source):
    width = psi.shape[1]
    chips = at.chips
    chip, core = place[0], place[1]
    row = lax.broadcasted_iota(jnp.int32, (width, width), 0)
    col = lax.broadcasted_iota(jnp.int32, (width, width), 1)
    zero = jnp.int32(0)

    def slot_of(sector):
        where = owner[sector]
        away = lax.rem(where // CORES - chip + chips, chips)
        away = jnp.where(away == at.far, chips - 1, jnp.where(away > at.far, away - 1, away))
        return away * CORES + lax.rem(where + core, CORES)

    def clear_slot(s, carry):
        base[s] = 0
        return carry

    def count(k, carry):
        slot = slot_of(lsec[k])
        rank[k] = base[slot]
        base[slot] = base[slot] + 1
        return carry

    def begin(s, first):
        members = base[s]
        base[s] = first
        return first + members

    def enter(k, carry):
        lists[at.origin + base[slot_of(lsec[k])] + rank[k]] = k
        return carry

    lax.fori_loop(0, at.sectors, clear_slot, 0)
    lax.fori_loop(0, at.count, count, 0)
    lax.fori_loop(0, at.sectors, begin, zero)
    lax.fori_loop(0, at.count, enter, 0)

    for part, (start, size, first) in enumerate(zip(at.starts, at.sizes, at.firsts)):
        def clear_pair(p, carry):
            lists[at.left + p] = 0
            for h in range(2):
                lists[at.right + 2 * p + h] = 0
                lists[at.position + 2 * p + h] = size
                source[2 * p + h] = 0
            return carry

        def pair_up(i, carry):
            pair, filled, before = carry
            k = lists[at.origin + start + i]
            left, right = lsec[k], rsec[k]
            same = (filled == 1) & (left == before) & (i != size // 2)
            pair = jnp.where(same, pair, pair + 1)
            filled = jnp.where(same, 2, 1)
            half = 2 * pair + filled - 1
            lists[at.left + pair] = slot_of(left)
            lists[at.right + half] = slot_of(right)
            lists[at.position + half] = i
            lists[at.rows + start + i] = live[left]
            lists[at.columns + start + i] = live[right]
            source[half] = k
            return pair, filled, left

        lax.fori_loop(first, first + at.pairs[part], clear_pair, 0)
        last, _, _ = lax.fori_loop(0, size, pair_up, (zero + first - 1, zero, zero - 1))
        groups = (last - first + DEPTH) // DEPTH
        lists[at.groups + part] = groups

        def fill(i, carry):
            for u in range(DEPTH):
                p = first + i * DEPTH + u
                for h in range(2):
                    k = source[2 * p + h]
                    mask = (row < live[lsec[k]]) & (col < live[rsec[k]])
                    block = psi[k]
                    halves[p, :, h * width:(h + 1) * width] = jnp.where(mask, block, jnp.zeros_like(block))
            return carry

        lax.fori_loop(0, groups, fill, 0)


def multiply_kernel(part, at, place, lists, halves, right, left, own, ahead, later, inner):
    width = halves.shape[1]
    rows = own.shape[1]
    channels = left.shape[1]
    first = at.firsts[part]
    groups = lists[at.groups + part]

    def one(group, side):
        for u in range(DEPTH):
            pair = first + group * DEPTH + u
            for h in range(2):
                slot = lists[at.right + 2 * pair + h]
                wide = jnp.concatenate([right[slot, w] for w in range(channels)], axis=1)
                block = halves[pair, :, h * width:(h + 1) * width]
                z = jnp.dot(block, wide, preferred_element_type=jnp.float32).astype(jnp.bfloat16)
                for w in range(channels):
                    inner[side * DEPTH + u, w * width:(w + 1) * width, h * width:(h + 1) * width] = (
                        z[:, w * width:(w + 1) * width]
                    )

    def two(group, side):
        for u in range(DEPTH):
            pair = first + group * DEPTH + u
            slot = lists[at.left + pair]
            second = lists[at.position + 2 * pair] >= at.sizes[part] // 2
            ways = (0, jnp.where(second, 2, 1), 3, jnp.where(second, 1, 2))
            wide = []
            for way in ways:
                start = pl.multiple_of((place[2] ^ way) * rows, rows)
                wide.append(jnp.concatenate([left[slot, w, pl.ds(start, rows), :] for w in range(channels)], axis=1))
            wide = jnp.concatenate(wide, axis=0)
            result = jnp.dot(wide, inner[side * DEPTH + u], preferred_element_type=jnp.float32).astype(jnp.bfloat16)
            for h in range(2):
                where = lists[at.position + 2 * pair + h]
                columns = slice(h * width, (h + 1) * width)
                own[where] = result[0:rows, columns]
                ahead[where] = result[rows:3 * rows, columns]
                later[where] = result[3 * rows:4 * rows, columns]

    def body(i, carry):
        one(2 * i + 1, 1)
        two(2 * i, 0)
        one(2 * i + 2, 0)
        two(2 * i + 1, 1)
        return carry

    one(0, 0)
    turns = (groups - 1) // 2
    lax.fori_loop(0, turns, body, 0)

    @pl.when(2 * turns + 1 == groups)
    def _():
        two(2 * turns, 0)

    @pl.when(2 * turns + 1 != groups)
    def _():
        one(2 * turns + 1, 1)
        two(2 * turns, 0)
        two(2 * turns + 1, 1)


def place_kernel(at, place, lists, *rest):
    out, totals = rest[-1], rest[:-1]
    rows, width = out.shape[1], out.shape[2]
    row = place[2] * rows + lax.broadcasted_iota(jnp.int32, (rows, width), 0)
    col = lax.broadcasted_iota(jnp.int32, (rows, width), 1)

    starts = [sum(t.shape[0] for t in totals[:i]) for i in range(len(totals))]
    for start, total in zip(starts, totals):
        def body(i, carry):
            blocks = []
            for u in range(BATCH):
                k = start + i * BATCH + u
                mask = (row < lists[at.rows + k]) & (col < lists[at.columns + k])
                block = total[i * BATCH + u].astype(jnp.float32)
                blocks.append(jnp.where(mask, block, jnp.zeros_like(block)).astype(jnp.bfloat16))
            for u in range(BATCH):
                out[lists[at.origin + start + i * BATCH + u]] = blocks[u]
            return carry

        lax.fori_loop(0, total.shape[0] // BATCH, body, 0)


def on_device(psi, left_env, right_env, left_sector, right_sector, sector_owner, sector_rows):
    nwave = lax.axis_size("wave")
    nenv = lax.axis_size("env")
    count, width = psi.shape[0], psi.shape[1]
    channels = left_env.shape[0]
    sectors = sector_owner.shape[0]
    chips = nwave // CORES
    rows = width // nenv
    wave = lax.axis_index("wave")
    env = lax.axis_index("env")
    place = jnp.stack([wave // CORES, wave % CORES, env]).astype(jnp.int32)

    up = [(i, (i + CORES) % nwave) for i in range(nwave)]
    down = [((i + CORES) % nwave, i) for i in range(nwave)]
    other = [(i, i ^ 1) for i in range(nwave)]
    at = Lists(count, sectors, chips)

    def swap(x):
        return lax.ppermute(x, "wave", other)

    def gate(*values):
        return lax.optimization_barrier(values)

    def ring(own):
        held = {0: own}
        rising = falling = own
        for r in range(1, (chips - 1) // 2 + 1):
            rising = lax.ppermute(rising, "wave", up)
            falling = lax.ppermute(falling, "wave", down)
            held[chips - r], held[r] = rising, falling
        return held, rising, falling

    def far(rising, falling, lo, hi):
        mid = (lo + hi) // 2
        return [lax.ppermute(rising[lo:mid], "wave", up), lax.ppermute(falling[mid:hi], "wave", down)]

    def far_pieces(last):
        return [jnp.concatenate(last), jnp.concatenate([swap(x) for x in last])]

    held, rising, falling = ring(jnp.concatenate([right_env[:, 0], left_env[:, 0]]))
    pieces = [piece for d in range(chips) if d in held for piece in (held[d], swap(held[d]))]
    right = [piece[:channels] for piece in pieces]
    near = jnp.stack([piece[channels:] for piece in pieces])
    if chips % 2 == 0:
        right += far_pieces(far(rising, falling, 0, channels))
        last = far(rising, falling, channels, 2 * channels)
    right = jnp.stack(right)

    lists, halves = pl.pallas_call(
        functools.partial(order_kernel, at),
        out_shape=(
            jax.ShapeDtypeStruct((at.length,), jnp.int32),
            jax.ShapeDtypeStruct((at.all_pairs, width, 2 * width), jnp.bfloat16),
        ),
        in_specs=[SMEM] * 5 + [VMEM],
        out_specs=(SMEM, VMEM),
        scratch_shapes=[pltpu.SMEM((n,), jnp.int32) for n in (sectors, count, 2 * at.all_pairs)],
        compiler_params=pltpu.CompilerParams(vmem_limit_bytes=2 * (psi.size + 2 * at.all_pairs * width * width) + (4 << 20)),
    )(place, left_sector[:, 0], right_sector[:, 0], sector_owner, sector_rows, psi)

    def multiply(part, right, left):
        need = right.size + left.size + halves.size + count * width * width
        need = 2 * (need + 4 * DEPTH * channels * width * width) + (8 << 20)
        return list(pl.pallas_call(
            functools.partial(multiply_kernel, part, at),
            out_shape=[
                jax.ShapeDtypeStruct((at.sizes[part] + 1, n * rows, width), jnp.bfloat16) for n in (1, 2, 1)
            ],
            in_specs=[SMEM] * 2 + [VMEM] * 3,
            out_specs=[VMEM] * 3,
            scratch_shapes=[pltpu.VMEM((2 * DEPTH, channels * width, 2 * width), jnp.bfloat16)],
            compiler_params=pltpu.CompilerParams(vmem_limit_bytes=min(need, 60 << 20)),
            cost_estimate=NO_COST,
        )(place, lists, halves, right, left))

    def pass_on(x, d):
        return lax.ppermute(x, "env", [(i, i ^ d) for i in range(nenv)])

    def exchange(part, parts):
        own, ahead, later = parts
        middle, end = at.sizes[part] // 2, at.sizes[part]
        wide = lambda x: x.astype(jnp.float32)
        totals = []
        arrived = [pass_on(ahead[0:middle], 1), pass_on(ahead[middle:end], 2)]
        for (lo, hi), first, d in zip(((0, middle), (middle, end)), arrived, (2, 1)):
            second = pass_on((wide(later[lo:hi]) + wide(first[:, rows:])).astype(jnp.bfloat16), d)
            totals.append((wide(own[lo:hi]) + wide(first[:, :rows]) + wide(second)).astype(jnp.bfloat16))
        return totals

    parts = multiply(0, right, near)
    if chips % 2 == 0:
        parts[0], *last = gate(parts[0], *last)
        whole = jnp.concatenate([near, jnp.stack(far_pieces(last))])
    else:
        whole = near
    terms = exchange(0, parts)
    for part in range(1, len(PARTS)):
        terms += exchange(part, multiply(part, right, whole))
    return pl.pallas_call(
        functools.partial(place_kernel, at),
        out_shape=jax.ShapeDtypeStruct((count, rows, width), jnp.bfloat16),
        in_specs=[SMEM] * 2 + [VMEM] * len(terms),
        out_specs=VMEM,
        compiler_params=pltpu.CompilerParams(vmem_limit_bytes=4 * count * rows * width + (4 << 20)),
        cost_estimate=NO_COST,
    )(place, lists, *terms)


def solution(mesh):
    return jax.shard_map(
        on_device,
        mesh=mesh,
        in_specs=(
            P("wave", None, None),
            P("env", "wave", None, None),
            P("env", "wave", None, None),
            P("wave", None),
            P("wave", None),
            P(),
            P(),
        ),
        out_specs=P("wave", "env", None),
        check_vma=False,
    )
```

```python
import functools

import jax
import jax.numpy as jnp
from jax import lax
from jax.experimental import pallas as pl
from jax.experimental.pallas import tpu as pltpu
from jax.sharding import PartitionSpec as P

CORES = 2
DEPTH = 3
PARTS = (2, 2)
BATCH = 8
NO_COST = pl.CostEstimate(flops=0, bytes_accessed=0, transcendentals=0)
SMEM = pl.BlockSpec(memory_space=pltpu.SMEM)
VMEM = pl.BlockSpec(memory_space=pltpu.VMEM)


class Lists:
    def __init__(self, count, sectors, chips):
        self.count = count
        self.sectors = sectors
        self.chips = chips
        self.sizes = [count // n for n in PARTS]
        self.starts = [sum(self.sizes[:i]) for i in range(len(PARTS))]
        self.pairs = [((n + min(sectors, n) + 2) // 2 + DEPTH - 1) // DEPTH * DEPTH for n in self.sizes]
        self.firsts = [sum(self.pairs[:i]) for i in range(len(PARTS))]
        self.all_pairs = sum(self.pairs)
        self.far = chips // 2 if chips % 2 == 0 else chips
        self.groups = 0
        self.left = self.groups + len(PARTS)
        self.right = self.left + self.all_pairs
        self.position = self.right + 2 * self.all_pairs
        self.origin = self.position + 2 * self.all_pairs
        self.rows = self.origin + count
        self.columns = self.rows + count
        self.length = self.columns + count


def order_kernel(at, place, lsec, rsec, owner, live, psi, lists, halves, base, rank, source):
    width = psi.shape[1]
    chips = at.chips
    chip, core = place[0], place[1]
    row = lax.broadcasted_iota(jnp.int32, (width, width), 0)
    col = lax.broadcasted_iota(jnp.int32, (width, width), 1)
    zero = jnp.int32(0)

    def slot_of(sector):
        where = owner[sector]
        away = lax.rem(where // CORES - chip + chips, chips)
        away = jnp.where(away == at.far, chips - 1, jnp.where(away > at.far, away - 1, away))
        return away * CORES + lax.rem(where + core, CORES)

    def clear_slot(s, carry):
        base[s] = 0
        return carry

    def count(k, carry):
        slot = slot_of(lsec[k])
        rank[k] = base[slot]
        base[slot] = base[slot] + 1
        return carry

    def begin(s, first):
        members = base[s]
        base[s] = first
        return first + members

    def enter(k, carry):
        lists[at.origin + base[slot_of(lsec[k])] + rank[k]] = k
        return carry

    lax.fori_loop(0, at.sectors, clear_slot, 0)
    lax.fori_loop(0, at.count, count, 0)
    lax.fori_loop(0, at.sectors, begin, zero)
    lax.fori_loop(0, at.count, enter, 0)

    for part, (start, size, first) in enumerate(zip(at.starts, at.sizes, at.firsts)):
        def clear_pair(p, carry):
            lists[at.left + p] = 0
            for h in range(2):
                lists[at.right + 2 * p + h] = 0
                lists[at.position + 2 * p + h] = size
                source[2 * p + h] = 0
            return carry

        def pair_up(i, carry):
            pair, filled, before = carry
            k = lists[at.origin + start + i]
            left, right = lsec[k], rsec[k]
            same = (filled == 1) & (left == before) & (i != size // 2)
            pair = jnp.where(same, pair, pair + 1)
            filled = jnp.where(same, 2, 1)
            half = 2 * pair + filled - 1
            lists[at.left + pair] = slot_of(left)
            lists[at.right + half] = slot_of(right)
            lists[at.position + half] = i
            lists[at.rows + start + i] = live[left]
            lists[at.columns + start + i] = live[right]
            source[half] = k
            return pair, filled, left

        lax.fori_loop(first, first + at.pairs[part], clear_pair, 0)
        last, _, _ = lax.fori_loop(0, size, pair_up, (zero + first - 1, zero, zero - 1))
        groups = (last - first + DEPTH) // DEPTH
        lists[at.groups + part] = groups

        def fill(i, carry):
            for u in range(DEPTH):
                p = first + i * DEPTH + u
                for h in range(2):
                    k = source[2 * p + h]
                    mask = (row < live[lsec[k]]) & (col < live[rsec[k]])
                    block = psi[k]
                    halves[p, :, h * width:(h + 1) * width] = jnp.where(mask, block, jnp.zeros_like(block))
            return carry

        lax.fori_loop(0, groups, fill, 0)


def multiply_kernel(part, at, place, lists, halves, right, left, own, ahead, later, inner):
    width = halves.shape[1]
    rows = own.shape[1]
    channels = left.shape[1]
    first = at.firsts[part]
    groups = lists[at.groups + part]

    def one(group, side):
        for u in range(DEPTH):
            pair = first + group * DEPTH + u
            for h in range(2):
                slot = lists[at.right + 2 * pair + h]
                wide = jnp.concatenate([right[slot, w] for w in range(channels)], axis=1)
                block = halves[pair, :, h * width:(h + 1) * width]
                z = jnp.dot(block, wide, preferred_element_type=jnp.float32).astype(jnp.bfloat16)
                for w in range(channels):
                    inner[side * DEPTH + u, w * width:(w + 1) * width, h * width:(h + 1) * width] = (
                        z[:, w * width:(w + 1) * width]
                    )

    def two(group, side):
        for u in range(DEPTH):
            pair = first + group * DEPTH + u
            slot = lists[at.left + pair]
            second = lists[at.position + 2 * pair] >= at.sizes[part] // 2
            ways = (0, jnp.where(second, 2, 1), 3, jnp.where(second, 1, 2))
            wide = []
            for way in ways:
                start = pl.multiple_of((place[2] ^ way) * rows, rows)
                wide.append(jnp.concatenate([left[slot, w, pl.ds(start, rows), :] for w in range(channels)], axis=1))
            wide = jnp.concatenate(wide, axis=0)
            result = jnp.dot(wide, inner[side * DEPTH + u], preferred_element_type=jnp.float32).astype(jnp.bfloat16)
            for h in range(2):
                where = lists[at.position + 2 * pair + h]
                columns = slice(h * width, (h + 1) * width)
                own[where] = result[0:rows, columns]
                ahead[where] = result[rows:3 * rows, columns]
                later[where] = result[3 * rows:4 * rows, columns]

    def body(i, carry):
        one(2 * i + 1, 1)
        two(2 * i, 0)
        one(2 * i + 2, 0)
        two(2 * i + 1, 1)
        return carry

    one(0, 0)
    turns = (groups - 1) // 2
    lax.fori_loop(0, turns, body, 0)

    @pl.when(2 * turns + 1 == groups)
    def _():
        two(2 * turns, 0)

    @pl.when(2 * turns + 1 != groups)
    def _():
        one(2 * turns + 1, 1)
        two(2 * turns, 0)
        two(2 * turns + 1, 1)


def place_kernel(at, place, lists, *rest):
    out, totals = rest[-1], rest[:-1]
    rows, width = out.shape[1], out.shape[2]
    row = place[2] * rows + lax.broadcasted_iota(jnp.int32, (rows, width), 0)
    col = lax.broadcasted_iota(jnp.int32, (rows, width), 1)

    starts = [sum(t.shape[0] for t in totals[:i]) for i in range(len(totals))]
    for start, total in zip(starts, totals):
        def body(i, carry):
            blocks = []
            for u in range(BATCH):
                k = start + i * BATCH + u
                mask = (row < lists[at.rows + k]) & (col < lists[at.columns + k])
                block = total[i * BATCH + u].astype(jnp.float32)
                blocks.append(jnp.where(mask, block, jnp.zeros_like(block)).astype(jnp.bfloat16))
            for u in range(BATCH):
                out[lists[at.origin + start + i * BATCH + u]] = blocks[u]
            return carry

        lax.fori_loop(0, total.shape[0] // BATCH, body, 0)


def on_device(psi, left_env, right_env, left_sector, right_sector, sector_owner, sector_rows):
    nwave = lax.axis_size("wave")
    nenv = lax.axis_size("env")
    count, width = psi.shape[0], psi.shape[1]
    channels = left_env.shape[0]
    sectors = sector_owner.shape[0]
    chips = nwave // CORES
    rows = width // nenv
    wave = lax.axis_index("wave")
    env = lax.axis_index("env")
    place = jnp.stack([wave // CORES, wave % CORES, env]).astype(jnp.int32)

    up = [(i, (i + CORES) % nwave) for i in range(nwave)]
    down = [((i + CORES) % nwave, i) for i in range(nwave)]
    other = [(i, i ^ 1) for i in range(nwave)]
    at = Lists(count, sectors, chips)

    def swap(x):
        return lax.ppermute(x, "wave", other)

    def gate(*values):
        return lax.optimization_barrier(values)

    def ring(own):
        held = {0: own}
        rising = falling = own
        for r in range(1, (chips - 1) // 2 + 1):
            rising = lax.ppermute(rising, "wave", up)
            falling = lax.ppermute(falling, "wave", down)
            held[chips - r], held[r] = rising, falling
        return held, rising, falling

    def far(rising, falling, lo, hi):
        mid = (lo + hi) // 2
        return [lax.ppermute(rising[lo:mid], "wave", up), lax.ppermute(falling[mid:hi], "wave", down)]

    def far_pieces(last):
        return [jnp.concatenate(last), jnp.concatenate([swap(x) for x in last])]

    held, rising, falling = ring(jnp.concatenate([right_env[:, 0], left_env[:, 0]]))
    pieces = [piece for d in range(chips) if d in held for piece in (held[d], swap(held[d]))]
    right = [piece[:channels] for piece in pieces]
    near = jnp.stack([piece[channels:] for piece in pieces])
    if chips % 2 == 0:
        right += far_pieces(far(rising, falling, 0, channels))
        last = far(rising, falling, channels, 2 * channels)
    right = jnp.stack(right)

    lists, halves = pl.pallas_call(
        functools.partial(order_kernel, at),
        out_shape=(
            jax.ShapeDtypeStruct((at.length,), jnp.int32),
            jax.ShapeDtypeStruct((at.all_pairs, width, 2 * width), jnp.bfloat16),
        ),
        in_specs=[SMEM] * 5 + [VMEM],
        out_specs=(SMEM, VMEM),
        scratch_shapes=[pltpu.SMEM((n,), jnp.int32) for n in (sectors, count, 2 * at.all_pairs)],
        compiler_params=pltpu.CompilerParams(vmem_limit_bytes=2 * (psi.size + 2 * at.all_pairs * width * width) + (4 << 20)),
    )(place, left_sector[:, 0], right_sector[:, 0], sector_owner, sector_rows, psi)

    def multiply(part, right, left):
        need = right.size + left.size + halves.size + count * width * width
        need = 2 * (need + 4 * DEPTH * channels * width * width) + (8 << 20)
        return list(pl.pallas_call(
            functools.partial(multiply_kernel, part, at),
            out_shape=[
                jax.ShapeDtypeStruct((at.sizes[part] + 1, n * rows, width), jnp.bfloat16) for n in (1, 2, 1)
            ],
            in_specs=[SMEM] * 2 + [VMEM] * 3,
            out_specs=[VMEM] * 3,
            scratch_shapes=[pltpu.VMEM((2 * DEPTH, channels * width, 2 * width), jnp.bfloat16)],
            compiler_params=pltpu.CompilerParams(vmem_limit_bytes=min(need, 60 << 20)),
            cost_estimate=NO_COST,
        )(place, lists, halves, right, left))

    def pass_on(x, d):
        return lax.ppermute(x, "env", [(i, i ^ d) for i in range(nenv)])

    def exchange(part, parts):
        own, ahead, later = parts
        middle, end = at.sizes[part] // 2, at.sizes[part]
        wide = lambda x: x.astype(jnp.float32)
        totals = []
        arrived = [pass_on(ahead[0:middle], 1), pass_on(ahead[middle:end], 2)]
        for (lo, hi), first, d in zip(((0, middle), (middle, end)), arrived, (2, 1)):
            second = pass_on((wide(later[lo:hi]) + wide(first[:, rows:])).astype(jnp.bfloat16), d)
            totals.append((wide(own[lo:hi]) + wide(first[:, :rows]) + wide(second)).astype(jnp.bfloat16))
        return totals

    parts = multiply(0, right, near)
    if chips % 2 == 0:
        parts[0], *last = gate(parts[0], *last)
        whole = jnp.concatenate([near, jnp.stack(far_pieces(last))])
    else:
        whole = near
    terms = exchange(0, parts)
    for part in range(1, len(PARTS)):
        terms += exchange(part, multiply(part, right, whole))
    return pl.pallas_call(
        functools.partial(place_kernel, at),
        out_shape=jax.ShapeDtypeStruct((count, rows, width), jnp.bfloat16),
        in_specs=[SMEM] * 2 + [VMEM] * len(terms),
        out_specs=VMEM,
        compiler_params=pltpu.CompilerParams(vmem_limit_bytes=4 * count * rows * width + (4 << 20)),
        cost_estimate=NO_COST,
    )(place, lists, *terms)


def solution(mesh):
    return jax.shard_map(
        on_device,
        mesh=mesh,
        in_specs=(
            P("wave", None, None),
            P("env", "wave", None, None),
            P("env", "wave", None, None),
            P("wave", None),
            P("wave", None),
            P(),
            P(),
        ),
        out_specs=P("wave", "env", None),
        check_vma=False,
    )
```
